32 devices in a mesh: groups: 2 (over y), rows: 4 (over z), tensor: 2 (over x), sub: 2 (over core).
Axes of the slice: x: 2, y: 2, z: 4, core: 2. Of those that a mesh axis runs over, the one named last changes fastest.
Arguments:
- features: bfloat16 [512, 24576], P(('groups', 'rows'), ('tensor', 'sub')), parts along dimension 0, may hold values from -6 to 6
- fc_weight: bfloat16 [24576, 4096], P(('tensor', 'sub'), 'rows'), may hold values from -0.0390625 to 0.0390625
- counts: int32 [8], P('groups'), parts along dimension 0, may hold values from 1 to 128, 256 in all
- order: int32 [512], P('groups'), parts along dimension 0, may hold values from 0 to 255, each once
- norm_gain: float32 [4096], replicated, may hold values from 0.1 to 1.9
- target: bfloat16 [1024, 4096], P(('groups', 'rows', 'tensor', 'sub')), parts along dimension 0, may hold values from -6 to 6
Outputs:
- fc_grad: float32 [49152, 4096], P(('groups', 'tensor', 'sub'), 'rows'), parts along dimension 0
- loss_slots: float32 [1024], P(('groups', 'rows', 'tensor', 'sub')), parts along dimension 0
The draws below stay inside these ranges and needn't reach their ends.
There are 2 independent parts, one for each index of `groups`. The reference program is written for one: setup_inputs(seed, part) draws one part's arguments, and reference() takes and returns one part's arrays. A program takes and returns all parts, laid end to end along the dimension named above; an argument that names none is the same for every part. Nothing has to cross between parts.
Inputs may be any that keep to these rules, and one draw needn't show every extreme that they name: counts sum to 256; the largest is exactly 128. `order`: each position appears exactly once.
All inputs are finite; a program needn't handle non-finite values.
Results may differ from the reference program's by a relative error of at most 0.0029.
Values may be sent and summed in bfloat16 or wider, within the bound.
A program may use at most 192 MiB of HBM per device.

```python
import math
import jax
import jax.numpy as jnp
import numpy as np
from jax import lax

D = 4096
IN = 24576
POSITIONS = 256
CAP = 128
N_ROWS = 4


def block_levels(own_key, dims, cuts, smallest, largest):
    factor_of = 1.0
    for axis_at, parts in cuts:
        steps = jax.random.uniform(jax.random.fold_in(jax.random.fold_in(own_key, 6), axis_at), (parts,), jnp.float32, smallest / len(cuts), largest / len(cuts))
        factor_of = factor_of * jnp.repeat(jnp.exp(steps), dims[axis_at] // parts).reshape((-1,) + (1,) * (len(dims) - 1 - axis_at))
    return factor_of


def profile(amount, total, reach, lean):
    portions = [(1 << 20) // math.isqrt(grade ** lean) + 1 for grade in range(2, amount + 1)]
    spare, given = total - reach - (amount - 1), [1] * (amount - 1)
    while spare > 0:
        free = [i for i in range(amount - 1) if given[i] < reach]
        pool, budget = sum([portions[i] for i in free]), spare
        for i in free:
            extra = min(reach - given[i], max(1, budget * portions[i] // pool), spare)
            given[i] = given[i] + extra
            spare = spare - extra
    return np.array([reach] + given)


def uneven(stream_key, number_of, total, reach, slope):
    if number_of == 2:
        one = jax.random.randint(stream_key, (), max(1, total - reach), min(reach, total - 1) + 1)
        return jnp.stack([one, total - one])
    lengths = jnp.asarray(profile(number_of, total, reach, slope), jnp.int32)
    pairs = (number_of - 1) // 2
    donor, receiver = lengths[1:1 + 2 * pairs:2], lengths[2:2 + 2 * pairs:2]
    room = jnp.minimum(donor - 1, reach - receiver)
    passed = jax.random.randint(jax.random.fold_in(stream_key, 1), (pairs,), 0, 1 << 20) % (room + 1)
    lengths = lengths.at[1:1 + 2 * pairs:2].set(donor - passed).at[2:2 + 2 * pairs:2].set(receiver + passed)
    return lengths[jax.random.permutation(jax.random.fold_in(stream_key, 2), number_of)]


def noise(stream_key, extent, spread, bound, split=(), held_as=jnp.bfloat16):
    level = block_levels(stream_key, extent, split, -0.22, 0.18) if split else 1.0
    values = jax.random.normal(stream_key, extent, jnp.float32) * spread * level
    return jnp.minimum(jnp.maximum(values, -bound), bound).astype(held_as)


def setup_inputs(seed: int = 0, part: int = 0) -> dict:
    key_of = jax.random.split(jax.random.key(seed), 7)
    own_keys = jax.random.split(jax.random.fold_in(key_of[6], part), 7)
    features = noise(own_keys[0], (POSITIONS, IN), 1.0, 6.0, ((0, 4), (1, 4)))
    fc_weight = noise(key_of[1], (IN, D), IN ** -0.5, 0.0390625, ((0, 4), (1, 4)))
    counts = uneven(own_keys[2], N_ROWS, POSITIONS, CAP, 2).astype(jnp.int32)
    order = jax.random.permutation(own_keys[3], POSITIONS).astype(jnp.int32)
    norm_gain = jnp.clip(1.0 + 0.18 * jax.random.normal(key_of[4], (D,), jnp.float32), 0.1, 1.9)
    target = noise(own_keys[5], (N_ROWS * CAP, D), 1.0, 6.0, ((0, 16),))
    return {"features": features, "fc_weight": fc_weight, "counts": counts, "order": order, "norm_gain": norm_gain, "target": target}


def slot_table(counts, order):
    total = order.shape[0]
    offsets = jnp.cumsum(counts) - counts
    index = jnp.arange(CAP, dtype=jnp.int32)
    live = index[None, :] < counts[:, None]
    spot = jnp.minimum(offsets[:, None] + index[None, :], total - 1).astype(jnp.int32)
    return (jnp.take(order, spot), live)

def reference(features, fc_weight, counts, order, norm_gain, target):
    total = order.shape[0]
    joined = jnp.dot(features, fc_weight, preferred_element_type=jnp.float32)
    slot_pos, live = slot_table(counts, order)
    flat_pos = slot_pos.reshape(-1).astype(jnp.int32)
    flat_live = live.reshape(-1)
    hidden = jnp.where(flat_live[:, None], jnp.take(joined, flat_pos, axis=0), jnp.float32(0))
    rstat = lax.rsqrt(lax.optimization_barrier(jnp.mean(hidden * hidden, axis=1, keepdims=True)) + 1e-06)
    normed = hidden * rstat * norm_gain
    err = normed - target.astype(jnp.float32)
    loss_slots = jnp.where(flat_live, lax.optimization_barrier(jnp.mean(err * err, axis=1)), jnp.float32(0))
    dnormed = jnp.where(flat_live[:, None], err, jnp.float32(0)) / math.sqrt(total)
    scaled = norm_gain * dnormed
    dhidden = rstat * scaled - hidden * rstat * rstat * rstat * lax.optimization_barrier(jnp.mean(scaled * hidden, axis=1, keepdims=True))
    dhidden = dhidden.astype(jnp.bfloat16)
    target_rows = jnp.where(flat_live, flat_pos, total).astype(jnp.int32)
    grad_rows = jnp.zeros((total, fc_weight.shape[1]), jnp.bfloat16).at[target_rows].set(dhidden, mode='drop')
    fc_grad = lax.dot_general(features, grad_rows, (((0,), (0,)), ((), ())), preferred_element_type=jnp.float32)
    return (fc_grad, loss_slots)
```

```python
import functools
import math

import jax
import jax.numpy as jnp
from jax import lax
from jax.experimental import pallas as pl
from jax.experimental.pallas import tpu as pltpu
from jax.sharding import PartitionSpec as P

MESH = pl.DeviceIdType.MESH
F32 = jnp.float32
BF16 = jnp.bfloat16
CHUNKS = 4


def kernel(
    R, T, S, direct,
    counts_ref, order_ref, gain_ref, feat_in, w_in, target_in,
    feat_out, grad_out, loss_out,
    feat, w, acc, rs, tall, hid, tsel, stats, ag, lp, lz, lm,
    w_sem, own_sem, out_sem, f_send, f_recv, rs_send, rs_recv,
    tz_send, tz_recv, tm_send, tm_recv, st_send, st_recv,
    ag_send, ag_recv, lz_send, lz_recv, lm_send, lm_recv, tl_sem,
):
    M = T * S
    rows = feat.shape[2]
    part = feat.shape[3]
    cols = w.shape[2]
    pm = rows // M
    mine = R * pm
    share = target_in.shape[0]
    cap = share * M
    total = order_ref.shape[1]
    z = lax.axis_index("rows")
    t = lax.axis_index("tensor")
    s_ = lax.axis_index("sub")
    m = t * S + s_

    def member(j):
        q = lax.rem(m + j, M)
        return q, {"tensor": q // S, "sub": lax.rem(q, S)}

    def zpeer(j):
        q = lax.rem(z + j, R)
        return q, {"rows": q}

    def each_z(body):
        if R <= 4:
            for j in range(1, R):
                body(j)
        else:
            @pl.loop(1, R)
            def _(j):
                body(j)

    def w_copy(q):
        return pltpu.make_async_copy(w_in.at[pl.ds(q * part, part)], w.at[q], w_sem.at[q])

    def own_copy(q):
        return pltpu.make_async_copy(
            feat_in.at[:, pl.ds(q * part, part)], feat.at[z, q], own_sem.at[q])

    for q in range(CHUNKS):
        own_copy(q).start()
    own_cols = pl.ds(pl.multiple_of(z * cols, 128), cols)
    own_t = pltpu.make_async_copy(target_in.at[:, own_cols], tall.at[m, z], tl_sem.at[0])
    own_t.start()
    for q in range(CHUNKS):
        w_copy(q).start()

    barrier = pltpu.get_barrier_semaphore()

    def hello(j):
        _, dev = zpeer(j)
        pl.semaphore_signal(barrier, inc=1, device_id=dev, device_id_type=MESH)

    each_z(hello)
    for j in range(1, M):
        _, dev = member(j)
        pl.semaphore_signal(barrier, inc=1, device_id=dev, device_id_type=MESH)
    pl.semaphore_wait(barrier, R - 1 + M - 1)

    def f_copy(way, s, q):
        to = jnp.clip(z - 1 if way == 0 else z + 1, 0, R - 1)
        return pltpu.make_async_remote_copy(
            src_ref=feat.at[s, q], dst_ref=feat.at[s, q],
            send_sem=f_send.at[way, s, q], recv_sem=f_recv.at[s, q],
            device_id={"rows": to}, device_id_type=MESH)

    def out_copy(s, q):
        return pltpu.make_async_copy(
            feat.at[s, q],
            feat_out.at[pl.ds(pl.multiple_of(s * rows, rows), rows), pl.ds(q * part, part)],
            out_sem.at[s, q])

    def tz_copy(src, dst, dev):
        columns = pl.ds(pl.multiple_of(dst * cols, 128), cols)
        return pltpu.make_async_remote_copy(
            src_ref=target_in.at[:, columns], dst_ref=tall.at[m, src],
            send_sem=tz_send.at[dst], recv_sem=tz_recv.at[src],
            device_id=dev, device_id_type=MESH)

    def tm_copy(src, dst, dev):
        return pltpu.make_async_remote_copy(
            src_ref=tall.at[src], dst_ref=tall.at[src],
            send_sem=tm_send.at[dst], recv_sem=tm_recv.at[src],
            device_id=dev, device_id_type=MESH)

    def rs_copy(s, src, dst, dev):
        return pltpu.make_async_remote_copy(
            src_ref=acc.at[s, pl.ds(pl.multiple_of(dst * pm, pm), pm)], dst_ref=rs.at[s, src],
            send_sem=rs_send.at[s, dst], recv_sem=rs_recv.at[s, src],
            device_id=dev, device_id_type=MESH)

    def st_copy(src, dst, dev):
        return pltpu.make_async_remote_copy(
            src_ref=stats.at[src], dst_ref=stats.at[src],
            send_sem=st_send.at[dst], recv_sem=st_recv.at[src],
            device_id=dev, device_id_type=MESH)

    def ag_copy(src, dst, dev):
        return pltpu.make_async_remote_copy(
            src_ref=ag.at[src], dst_ref=ag.at[src],
            send_sem=ag_send.at[dst], recv_sem=ag_recv.at[src],
            device_id=dev, device_id_type=MESH)

    def lz_copy(src, dst, dev):
        return pltpu.make_async_remote_copy(
            src_ref=lp.at[dst], dst_ref=lz.at[src],
            send_sem=lz_send.at[dst], recv_sem=lz_recv.at[src],
            device_id=dev, device_id_type=MESH)

    def lm_copy(src, dst, dev):
        return pltpu.make_async_remote_copy(
            src_ref=lm.at[src], dst_ref=lm.at[src],
            send_sem=lm_send.at[dst], recv_sem=lm_recv.at[src],
            device_id=dev, device_id_type=MESH)

    for q in range(CHUNKS):
        own_copy(q).wait()

        @pl.when(z > 0)
        def _():
            f_copy(0, z, q).start()

        @pl.when(z < R - 1)
        def _():
            f_copy(1, z, q).start()

        out_copy(z, q).start()

    def send_target(j):
        dst, dev = zpeer(j)
        tz_copy(z, dst, dev).start()

    each_z(send_target)

    def multiply(s, q):
        piece = jnp.dot(feat[s, q], w[q], preferred_element_type=F32)
        if q == 0:
            acc[s] = piece
        else:
            acc[s] += piece

    def send_sums(s):
        for j in range(1, M):
            dst, dev = member(j)
            rs_copy(s, m, dst, dev).start()

    for q in range(CHUNKS):
        w_copy(q).wait()
        multiply(z, q)
    send_sums(z)

    def step(d):
        left, right = z - d, z + d
        for q in range(CHUNKS):
            @pl.when(right < R)
            def _():
                f_copy(0, right, q).wait_recv()

                @pl.when(z > 0)
                def _():
                    f_copy(0, right, q).start()

                out_copy(right, q).start()

            @pl.when(left >= 0)
            def _():
                f_copy(1, left, q).wait_recv()

                @pl.when(z < R - 1)
                def _():
                    f_copy(1, left, q).start()

                out_copy(left, q).start()
                multiply(left, q)

            @pl.when(right < R)
            def _():
                multiply(right, q)

        @pl.when(left >= 0)
        def _():
            send_sums(left)

        @pl.when(right < R)
        def _():
            send_sums(right)

    def target_out():
        own_t.wait()

        def arrived(j):
            src, dev = zpeer(j)
            tz_copy(src, z, dev).wait_recv()

        each_z(arrived)
        for j in range(1, M):
            dst, dev = member(j)
            tm_copy(m, dst, dev).start()

    step(1)
    target_out()

    row = lax.broadcasted_iota(jnp.int32, (mine, total), 0)
    position = (row // pm) * rows + m * pm + lax.rem(row, pm)
    rank = lax.broadcasted_iota(jnp.int32, (1, total), 1)
    trainer = jnp.zeros((1, total), jnp.int32)
    start = jnp.zeros((1, total), jnp.int32)
    end = jnp.int32(0)
    for r in range(R):
        n = counts_ref[r]
        end = end + n
        past = rank >= end
        trainer = trainer + jnp.where(past, 1, 0)
        start = start + jnp.where(past, n, 0)
    natural = trainer * cap + rank - start
    slot = jnp.sum(jnp.where(order_ref[...] == position, natural, 0), axis=1, keepdims=True)

    def step_loop(d, c):
        step(d)
        return c

    if R > 3:
        lax.fori_loop(2, R - 1, step_loop, 0)

    for j in range(1, M):
        src, dev = member(j)
        tm_copy(src, m, dev).wait_recv()
    trn = slot // cap
    inside = slot - trn * cap
    owner = inside // share
    place = owner * (R * share) + trn * share + (inside - owner * share)
    seat = lax.broadcasted_iota(jnp.int32, (mine, M * R * share), 1)
    pick = jnp.where(seat == place, F32(1), F32(0)).astype(BF16)
    tsel[...] = jnp.dot(
        pick, tall[...].reshape(M * R * share, cols), preferred_element_type=F32)

    if R > 2:
        step(R - 1)

    gain = gain_ref[:, own_cols]
    lane = lax.broadcasted_iota(jnp.int32, (pm, 128), 1)

    def collect(s, c):
        h = acc[s, pl.ds(pl.multiple_of(m * pm, pm), pm)]
        for j in range(1, M):
            src, dev = member(j)
            rs_copy(s, src, m, dev).wait_recv()
            h = h + rs[s, src]
        here = pl.ds(pl.multiple_of(s * pm, pm), pm)
        hid[here] = h
        gh = gain * h
        a = jnp.sum(h * h, axis=1, keepdims=True)
        b = jnp.sum(gh * gh, axis=1, keepdims=True)
        e = jnp.sum(gh * tsel[here], axis=1, keepdims=True)
        stats[z, here] = jnp.where(lane == 0, a, jnp.where(lane == 1, b, e))
        return c

    lax.fori_loop(0, R, collect, 0)

    def send_stats(j):
        dst, dev = zpeer(j)
        st_copy(z, dst, dev).start()

    each_z(send_stats)

    def got_stats(j):
        src, dev = zpeer(j)
        st_copy(src, z, dev).wait_recv()

    each_z(got_stats)
    summed = jnp.sum(stats[...], axis=0)
    depth = R * cols
    a, b, e = summed[:, 0:1], summed[:, 1:2], summed[:, 2:3]
    rstat = lax.rsqrt(a / depth + 1e-06)
    scale = 1.0 / math.sqrt(total)
    dotted = (rstat * b - e) * (scale / depth)
    h = hid[...]
    err = h * rstat * gain - tsel[...]
    dh = rstat * (gain * (err * scale)) - h * (rstat * rstat * rstat * dotted)
    ag[m] = dh.astype(BF16)
    for j in range(1, M):
        dst, dev = member(j)
        ag_copy(m, dst, dev).start()

    loss = jnp.sum(err * err, axis=1, keepdims=True) / depth
    seat1 = lax.broadcasted_iota(jnp.int32, (mine, cap), 1)

    def scatter(r, c):
        one = jnp.sum(
            jnp.where(slot - r * cap == seat1, loss, F32(0)), axis=0, keepdims=True)
        lp[r] = jnp.broadcast_to(one, (8, cap))
        return c

    lax.fori_loop(0, R, scatter, 0)

    def send_loss(j):
        dst, dev = zpeer(j)
        lz_copy(z, dst, dev).start()

    each_z(send_loss)
    lz[z] = lp[z]

    def got_loss(j):
        src, dev = zpeer(j)
        lz_copy(src, z, dev).wait_recv()

    each_z(got_loss)
    lm[m] = jnp.sum(lz[...], axis=0)
    for j in range(1, M):
        dst, dev = member(j)
        lm_copy(m, dst, dev).start()

    for j in range(1, M):
        src, dev = member(j)
        ag_copy(src, m, dev).wait_recv()
    if direct:
        for q in range(M):
            for s in range(R):
                grad_out[s * rows + q * pm:s * rows + (q + 1) * pm] = ag[q, s * pm:(s + 1) * pm]
    else:
        grad_out[...] = ag[...]
    for j in range(1, M):
        src, dev = member(j)
        lm_copy(src, m, dev).wait_recv()
    loss_out[...] = jnp.sum(lm[...], axis=0)

    def sent(s, c):
        for q in range(CHUNKS):
            out_copy(s, q).wait()

            @pl.when(jnp.logical_and(s >= z, z > 0))
            def _():
                f_copy(0, s, q).wait_send()

            @pl.when(jnp.logical_and(s <= z, z < R - 1))
            def _():
                f_copy(1, s, q).wait_send()

        for j in range(1, M):
            dst, dev = member(j)
            rs_copy(s, m, dst, dev).wait_send()
        return c

    lax.fori_loop(0, R, sent, 0)
    for j in range(1, M):
        dst, dev = member(j)
        tm_copy(m, dst, dev).wait_send()
        ag_copy(m, dst, dev).wait_send()
        lm_copy(m, dst, dev).wait_send()

    def sent_z(j):
        dst, dev = zpeer(j)
        tz_copy(z, dst, dev).wait_send()
        st_copy(z, dst, dev).wait_send()
        lz_copy(z, dst, dev).wait_send()

    each_z(sent_z)


def on_device(features, fc_weight, counts, order, norm_gain, target):
    R = lax.axis_size("rows")
    T = lax.axis_size("tensor")
    S = lax.axis_size("sub")
    M = T * S
    rows, depth = features.shape
    cols = fc_weight.shape[1]
    total = order.shape[0]
    share = target.shape[0]
    cap = share * M
    part = depth // CHUNKS
    pm = rows // M
    mine = R * pm
    direct = pm % 16 == 0
    any_ = pl.BlockSpec(memory_space=pl.ANY)
    vmem = pl.BlockSpec(memory_space=pltpu.VMEM)
    smem = pl.BlockSpec(memory_space=pltpu.SMEM)
    dma = pltpu.SemaphoreType.DMA
    grad_shape = (total, cols) if direct else (M, mine, cols)
    all_features, grad, loss = pl.pallas_call(
        functools.partial(kernel, R, T, S, direct),
        out_shape=(
            jax.ShapeDtypeStruct((total, depth), BF16),
            jax.ShapeDtypeStruct(grad_shape, BF16),
            jax.ShapeDtypeStruct((8, cap), F32),
        ),
        in_specs=[smem, vmem, vmem, any_, any_, any_],
        out_specs=(any_, vmem, vmem),
        scratch_shapes=[
            pltpu.VMEM((R, CHUNKS, rows, part), BF16),
            pltpu.VMEM((CHUNKS, part, cols), BF16),
            pltpu.VMEM((R, rows, cols), F32),
            pltpu.VMEM((R, M, pm, cols), F32),
            pltpu.VMEM((M, R, share, cols), BF16),
            pltpu.VMEM((mine, cols), F32),
            pltpu.VMEM((mine, cols), F32),
            pltpu.VMEM((R, mine, 128), F32),
            pltpu.VMEM((M, mine, cols), BF16),
            pltpu.VMEM((R, 8, cap), F32),
            pltpu.VMEM((R, 8, cap), F32),
            pltpu.VMEM((M, 8, cap), F32),
            dma((CHUNKS,)), dma((CHUNKS,)), dma((R, CHUNKS)),
            dma((2, R, CHUNKS)), dma((R, CHUNKS)),
            dma((R, M)), dma((R, M)),
            dma((R,)), dma((R,)), dma((M,)), dma((M,)),
            dma((R,)), dma((R,)), dma((M,)), dma((M,)),
            dma((R,)), dma((R,)), dma((M,)), dma((M,)), dma((1,)),
        ],
        compiler_params=pltpu.CompilerParams(
            collective_id=0, has_side_effects=True, vmem_limit_bytes=48 * 1024 * 1024),
        name="gather_join_norm",
    )(counts, order[None, :], norm_gain[None, :], features, fc_weight, target)
    if not direct:
        grad = grad.reshape(M, R, pm, cols).transpose(1, 0, 2, 3).reshape(total, cols)
    member = lax.axis_index("tensor") * S + lax.axis_index("sub")
    loss_slots = lax.dynamic_slice_in_dim(loss[0], member * share, share, 0)
    fc_grad = lax.dot_general(
        all_features, grad, (((0,), (0,)), ((), ())), preferred_element_type=F32)
    return (fc_grad, loss_slots)


def solution(mesh):
    return jax.shard_map(
        on_device,
        mesh=mesh,
        in_specs=(
            P(("groups", "rows"), ("tensor", "sub")),
            P(("tensor", "sub"), "rows"),
            P("groups"),
            P("groups"),
            P(),
            P(("groups", "rows", "tensor", "sub"), None),
        ),
        out_specs=(P(("groups", "tensor", "sub"), "rows"), P(("groups", "rows", "tensor", "sub"))),
        check_vma=False,
    )
```

```python
import functools
import math

import jax
import jax.numpy as jnp
from jax import lax
from jax.experimental import pallas as pl
from jax.experimental.pallas import tpu as pltpu
from jax.sharding import PartitionSpec as P

MESH = pl.DeviceIdType.MESH
F32 = jnp.float32
BF16 = jnp.bfloat16
CHUNKS = 4


def kernel(
    R, T, S,
    counts_in, order_in, gain_in, feat_in, w_in, target_in,
    feat_out, grad_out, loss_out,
    counts_ref, order_ref, gain_ref,
    feat, w, acc, rs, xs, tall, hid, tsel, rowsum, stats, ag, lp, lz, lm,
    w_sem, own_sem, out_sem, f_send, f_recv, rs_send, rs_recv, xs_send, xs_recv,
    tz_send, tz_recv, tm_send, tm_recv, st_send, st_recv,
    ag_send, ag_recv, lz_send, lz_recv, lm_send, lm_recv, tl_sem,
):
    M = T * S
    rows = feat.shape[2]
    part = feat.shape[3]
    cols = w.shape[2]
    pm = rows // S
    mine = R * pm
    share = target_in.shape[0]
    cap = share * M
    total = order_in.shape[1]
    z = lax.axis_index("rows")
    t = lax.axis_index("tensor")
    s_ = lax.axis_index("sub")
    m = t * S + s_

    def member(j):
        q = lax.rem(m + j, M)
        return q, {"tensor": q // S, "sub": lax.rem(q, S)}

    def core(j):
        q = lax.rem(s_ + j, S)
        return q, {"sub": q}

    def across(j):
        q = lax.rem(t + j, T)
        return q, {"tensor": q}

    def zpeer(j):
        q = lax.rem(z + j, R)
        return q, {"rows": q}

    def each_z(body):
        if R <= 4:
            for j in range(1, R):
                body(j)
        else:
            @pl.loop(1, R)
            def _(j):
                body(j)

    def w_copy(q):
        return pltpu.make_async_copy(w_in.at[pl.ds(q * part, part)], w.at[q], w_sem.at[q])

    def own_copy(q):
        return pltpu.make_async_copy(
            feat_in.at[:, pl.ds(q * part, part)], feat.at[z, q], own_sem.at[q])

    for q in range(CHUNKS):
        own_copy(q).start()
    own_cols = pl.ds(pl.multiple_of(z * cols, 128), cols)
    own_t = pltpu.make_async_copy(target_in.at[:, own_cols], tall.at[m, z], tl_sem.at[0])
    own_t.start()
    small = (
        pltpu.make_async_copy(counts_in, counts_ref, tl_sem.at[1]),
        pltpu.make_async_copy(order_in, order_ref, tl_sem.at[2]),
        pltpu.make_async_copy(gain_in.at[:, own_cols], gain_ref, tl_sem.at[3]),
    )
    for c in small:
        c.start()
    for q in range(CHUNKS):
        w_copy(q).start()

    barrier = pltpu.get_barrier_semaphore()

    def hello(j):
        _, dev = zpeer(j)
        pl.semaphore_signal(barrier, inc=1, device_id=dev, device_id_type=MESH)

    each_z(hello)
    for j in range(1, M):
        _, dev = member(j)
        pl.semaphore_signal(barrier, inc=1, device_id=dev, device_id_type=MESH)
    pl.semaphore_wait(barrier, R - 1 + M - 1)

    def f_copy(way, s, q):
        to = jnp.clip(z - 1 if way == 0 else z + 1, 0, R - 1)
        return pltpu.make_async_remote_copy(
            src_ref=feat.at[s, q], dst_ref=feat.at[s, q],
            send_sem=f_send.at[way, s, q], recv_sem=f_recv.at[s, q],
            device_id={"rows": to}, device_id_type=MESH)

    def out_copy(s, q):
        return pltpu.make_async_copy(
            feat.at[s, q],
            feat_out.at[pl.ds(pl.multiple_of(s * rows, rows), rows), pl.ds(q * part, part)],
            out_sem.at[s, q])

    def tz_copy(src, dst, dev):
        columns = pl.ds(pl.multiple_of(dst * cols, 128), cols)
        return pltpu.make_async_remote_copy(
            src_ref=target_in.at[:, columns], dst_ref=tall.at[m, src],
            send_sem=tz_send.at[dst], recv_sem=tz_recv.at[src],
            device_id=dev, device_id_type=MESH)

    def tm_copy(src, dst, dev):
        return pltpu.make_async_remote_copy(
            src_ref=tall.at[src], dst_ref=tall.at[src],
            send_sem=tm_send.at[dst], recv_sem=tm_recv.at[src],
            device_id=dev, device_id_type=MESH)

    def rs_copy(s, src, dst, dev):
        return pltpu.make_async_remote_copy(
            src_ref=acc.at[s, pl.ds(pl.multiple_of(dst * pm, pm), pm)], dst_ref=rs.at[s, src],
            send_sem=rs_send.at[s, dst], recv_sem=rs_recv.at[s, src],
            device_id=dev, device_id_type=MESH)

    def xs_copy(s, src, dst, dev):
        return pltpu.make_async_remote_copy(
            src_ref=xs.at[s, src], dst_ref=xs.at[s, src],
            send_sem=xs_send.at[s, dst], recv_sem=xs_recv.at[s, src],
            device_id=dev, device_id_type=MESH)

    def st_copy(src, dst, dev):
        return pltpu.make_async_remote_copy(
            src_ref=stats.at[src], dst_ref=stats.at[src],
            send_sem=st_send.at[dst], recv_sem=st_recv.at[src],
            device_id=dev, device_id_type=MESH)

    def ag_copy(src, dst, dev):
        return pltpu.make_async_remote_copy(
            src_ref=ag.at[src], dst_ref=ag.at[src],
            send_sem=ag_send.at[dst], recv_sem=ag_recv.at[src],
            device_id=dev, device_id_type=MESH)

    def lz_copy(src, dst, dev):
        return pltpu.make_async_remote_copy(
            src_ref=lp.at[dst], dst_ref=lz.at[src],
            send_sem=lz_send.at[dst], recv_sem=lz_recv.at[src],
            device_id=dev, device_id_type=MESH)

    def lm_copy(src, dst, dev):
        return pltpu.make_async_remote_copy(
            src_ref=lm.at[src], dst_ref=lm.at[src],
            send_sem=lm_send.at[dst], recv_sem=lm_recv.at[src],
            device_id=dev, device_id_type=MESH)

    for q in range(CHUNKS):
        own_copy(q).wait()

        @pl.when(z > 0)
        def _():
            f_copy(0, z, q).start()

        @pl.when(z < R - 1)
        def _():
            f_copy(1, z, q).start()

        out_copy(z, q).start()

    def send_target(j):
        dst, dev = zpeer(j)
        tz_copy(z, dst, dev).start()

    each_z(send_target)

    def multiply(s, q):
        piece = jnp.dot(feat[s, q], w[q], preferred_element_type=F32)
        if q == 0:
            acc[s] = piece
        else:
            acc[s] += piece

    def send_sums(s):
        for j in range(1, S):
            dst, dev = core(j)
            rs_copy(s, s_, dst, dev).start()

    def cross(s):
        h = acc[s, pl.ds(pl.multiple_of(s_ * pm, pm), pm)]
        for j in range(1, S):
            src, dev = core(j)
            rs_copy(s, src, s_, dev).wait_recv()
            h = h + rs[s, src]
        xs[s, t] = h
        for j in range(1, T):
            dst, dev = across(j)
            xs_copy(s, t, dst, dev).start()

    def cross_step(d):
        if isinstance(d, int) and d == 0:
            cross(z)
            return

        @pl.when(z - d >= 0)
        def _():
            cross(z - d)

        @pl.when(z + d < R)
        def _():
            cross(z + d)

    for q in range(CHUNKS):
        w_copy(q).wait()
        multiply(z, q)
    send_sums(z)

    def step(d):
        left, right = z - d, z + d
        for q in range(CHUNKS):
            @pl.when(right < R)
            def _():
                f_copy(0, right, q).wait_recv()

                @pl.when(z > 0)
                def _():
                    f_copy(0, right, q).start()

                out_copy(right, q).start()

            @pl.when(left >= 0)
            def _():
                f_copy(1, left, q).wait_recv()

                @pl.when(z < R - 1)
                def _():
                    f_copy(1, left, q).start()

                out_copy(left, q).start()
                multiply(left, q)

            @pl.when(right < R)
            def _():
                multiply(right, q)

            if q == 0:
                cross_step(d - 1)

        @pl.when(left >= 0)
        def _():
            send_sums(left)

        @pl.when(right < R)
        def _():
            send_sums(right)

    def target_out():
        own_t.wait()

        def arrived(j):
            src, dev = zpeer(j)
            tz_copy(src, z, dev).wait_recv()

        each_z(arrived)
        for j in range(1, M):
            dst, dev = member(j)
            tm_copy(m, dst, dev).start()

    step(1)
    for c in small:
        c.wait()
    target_out()

    row = lax.broadcasted_iota(jnp.int32, (mine, total), 0)
    position = (row // pm) * rows + s_ * pm + lax.rem(row, pm)
    rank = lax.broadcasted_iota(jnp.int32, (1, total), 1)
    trainer = jnp.zeros((1, total), jnp.int32)
    start = jnp.zeros((1, total), jnp.int32)
    end = jnp.int32(0)
    for r in range(R):
        n = counts_ref[r]
        end = end + n
        past = rank >= end
        trainer = trainer + jnp.where(past, 1, 0)
        start = start + jnp.where(past, n, 0)
    natural = trainer * cap + rank - start
    slot = jnp.sum(jnp.where(order_ref[...] == position, natural, 0), axis=1, keepdims=True)

    def step_loop(d, c):
        step(d)
        return c

    if R > 3:
        lax.fori_loop(2, R - 1, step_loop, 0)

    for j in range(1, M):
        src, dev = member(j)
        tm_copy(src, m, dev).wait_recv()
    trn = slot // cap
    inside = slot - trn * cap
    owner = inside // share
    place = owner * (R * share) + trn * share + (inside - owner * share)
    seat = lax.broadcasted_iota(jnp.int32, (mine, M * R * share), 1)
    pick = jnp.where(seat == place, F32(1), F32(0)).astype(BF16)
    tsel[...] = jnp.dot(
        pick, tall[...].reshape(M * R * share, cols), preferred_element_type=F32)

    if R > 2:
        step(R - 1)
    cross_step(R - 1)

    gain = gain_ref[...]
    lane = lax.broadcasted_iota(jnp.int32, (pm, 128), 1)

    def collect(s, c):
        for j in range(1, T):
            src, dev = across(j)
            xs_copy(s, src, t, dev).wait_recv()
        h = xs[s, 0]
        for q in range(1, T):
            h = h + xs[s, q]
        here = pl.ds(pl.multiple_of(s * pm, pm), pm)
        hid[here] = h
        gh = gain * h
        a = jnp.sum(h * h, axis=1, keepdims=True)
        b = jnp.sum(gh * gh, axis=1, keepdims=True)
        e = jnp.sum(gh * tsel[here], axis=1, keepdims=True)
        rowsum[here] = jnp.where(lane == 0, a, jnp.where(lane == 1, b, e))
        return c

    lax.fori_loop(0, R, collect, 0)

    stats[z] = rowsum[...].T[0:8]

    def send_stats(j):
        dst, dev = zpeer(j)
        st_copy(z, dst, dev).start()

    each_z(send_stats)

    def got_stats(j):
        src, dev = zpeer(j)
        st_copy(src, z, dev).wait_recv()

    each_z(got_stats)
    summed = jnp.sum(stats[...], axis=0)
    depth = R * cols
    a, b, e = summed[0:1], summed[1:2], summed[2:3]
    rstat = lax.rsqrt(a / depth + 1e-06)
    scale = 1.0 / math.sqrt(total)
    dotted = (rstat * b - e) * (scale / depth)
    line = lax.broadcasted_iota(jnp.int32, (128, mine), 0)
    factor = jnp.where(line == 0, rstat, rstat * rstat * rstat * dotted).T
    rstat, pull = factor[:, 0:1], factor[:, 1:2]
    h = hid[...]
    err = h * rstat * gain - tsel[...]
    dh = rstat * (gain * (err * scale)) - h * pull
    ag[s_] = dh.astype(BF16)
    for j in range(1, S):
        dst, dev = core(j)
        ag_copy(s_, dst, dev).start()

    loss = jnp.sum(err * err, axis=1, keepdims=True) / depth
    seat1 = lax.broadcasted_iota(jnp.int32, (mine, cap), 1)

    def scatter(r, c):
        one = jnp.sum(
            jnp.where(slot - r * cap == seat1, loss, F32(0)), axis=0, keepdims=True)
        lp[r] = jnp.broadcast_to(one, (8, cap))
        return c

    lax.fori_loop(0, R, scatter, 0)

    def send_loss(j):
        dst, dev = zpeer(j)
        lz_copy(z, dst, dev).start()

    each_z(send_loss)
    lz[z] = lp[z]

    def got_loss(j):
        src, dev = zpeer(j)
        lz_copy(src, z, dev).wait_recv()

    each_z(got_loss)
    lm[s_] = jnp.sum(lz[...], axis=0)
    for j in range(1, S):
        dst, dev = core(j)
        lm_copy(s_, dst, dev).start()

    for j in range(1, S):
        src, dev = core(j)
        ag_copy(src, s_, dev).wait_recv()
    for q in range(S):
        for s in range(R):
            grad_out[s * rows + q * pm:s * rows + (q + 1) * pm] = ag[q, s * pm:(s + 1) * pm]
    for j in range(1, S):
        src, dev = core(j)
        lm_copy(src, s_, dev).wait_recv()
    loss_out[...] = jnp.sum(lm[...], axis=0)

    def sent(s, c):
        for q in range(CHUNKS):
            out_copy(s, q).wait()

            @pl.when(jnp.logical_and(s >= z, z > 0))
            def _():
                f_copy(0, s, q).wait_send()

            @pl.when(jnp.logical_and(s <= z, z < R - 1))
            def _():
                f_copy(1, s, q).wait_send()

        for j in range(1, S):
            dst, dev = core(j)
            rs_copy(s, s_, dst, dev).wait_send()
        for j in range(1, T):
            dst, dev = across(j)
            xs_copy(s, t, dst, dev).wait_send()
        return c

    lax.fori_loop(0, R, sent, 0)
    for j in range(1, M):
        dst, dev = member(j)
        tm_copy(m, dst, dev).wait_send()
    for j in range(1, S):
        dst, dev = core(j)
        ag_copy(s_, dst, dev).wait_send()
        lm_copy(s_, dst, dev).wait_send()

    def sent_z(j):
        dst, dev = zpeer(j)
        tz_copy(z, dst, dev).wait_send()
        st_copy(z, dst, dev).wait_send()
        lz_copy(z, dst, dev).wait_send()

    each_z(sent_z)


def outer(f_ref, g_ref, out_ref):
    out_ref[...] = lax.dot_general(
        f_ref[...], g_ref[...], (((0,), (0,)), ((), ())), preferred_element_type=F32)


def on_device(features, fc_weight, counts, order, norm_gain, target):
    R = lax.axis_size("rows")
    T = lax.axis_size("tensor")
    S = lax.axis_size("sub")
    M = T * S
    rows, depth = features.shape
    cols = fc_weight.shape[1]
    total = order.shape[0]
    share = target.shape[0]
    cap = share * M
    part = depth // CHUNKS
    pm = rows // S
    mine = R * pm
    any_ = pl.BlockSpec(memory_space=pl.ANY)
    hbm = pl.BlockSpec(memory_space=pltpu.HBM)
    vmem = pl.BlockSpec(memory_space=pltpu.VMEM)
    dma = pltpu.SemaphoreType.DMA
    all_features, grad, loss = pl.pallas_call(
        functools.partial(kernel, R, T, S),
        out_shape=(
            jax.ShapeDtypeStruct((total, depth), BF16),
            jax.ShapeDtypeStruct((total, cols), BF16),
            jax.ShapeDtypeStruct((8, cap), F32),
        ),
        in_specs=[hbm] * 6,
        out_specs=(any_, vmem, vmem),
        scratch_shapes=[
            pltpu.SMEM((R,), jnp.int32),
            pltpu.VMEM((1, total), jnp.int32),
            pltpu.VMEM((1, cols), F32),
            pltpu.VMEM((R, CHUNKS, rows, part), BF16),
            pltpu.VMEM((CHUNKS, part, cols), BF16),
            pltpu.VMEM((R, rows, cols), F32),
            pltpu.VMEM((R, S, pm, cols), F32),
            pltpu.VMEM((R, T, pm, cols), F32),
            pltpu.VMEM((M, R, share, cols), BF16),
            pltpu.VMEM((mine, cols), F32),
            pltpu.VMEM((mine, cols), F32),
            pltpu.VMEM((mine, 128), F32),
            pltpu.VMEM((R, 8, mine), F32),
            pltpu.VMEM((S, mine, cols), BF16),
            pltpu.VMEM((R, 8, cap), F32),
            pltpu.VMEM((R, 8, cap), F32),
            pltpu.VMEM((S, 8, cap), F32),
            dma((CHUNKS,)), dma((CHUNKS,)), dma((R, CHUNKS)),
            dma((2, R, CHUNKS)), dma((R, CHUNKS)),
            dma((R, S)), dma((R, S)), dma((R, T)), dma((R, T)),
            dma((R,)), dma((R,)), dma((M,)), dma((M,)),
            dma((R,)), dma((R,)), dma((S,)), dma((S,)),
            dma((R,)), dma((R,)), dma((S,)), dma((S,)), dma((4,)),
        ],
        compiler_params=pltpu.CompilerParams(
            collective_id=0, has_side_effects=True, vmem_limit_bytes=48 * 1024 * 1024),
        name="gather_join_norm",
    )(counts, order[None, :], norm_gain[None, :], features, fc_weight, target)
    member = lax.axis_index("tensor") * S + lax.axis_index("sub")
    loss_slots = lax.dynamic_slice_in_dim(loss[0], member * share, share, 0)
    tile = depth // 12
    fc_grad = pl.pallas_call(
        outer,
        grid=(depth // tile,),
        out_shape=jax.ShapeDtypeStruct((depth, cols), F32),
        in_specs=[
            pl.BlockSpec((total, tile), lambda i: (0, i)),
            pl.BlockSpec((total, cols), lambda i: (0, 0)),
        ],
        out_specs=pl.BlockSpec((tile, cols), lambda i: (i, 0)),
        compiler_params=pltpu.CompilerParams(vmem_limit_bytes=32 * 1024 * 1024),
        name="weight_gradient",
    )(all_features, grad)
    return (fc_grad, loss_slots)


def solution(mesh):
    return jax.shard_map(
        on_device,
        mesh=mesh,
        in_specs=(
            P(("groups", "rows"), ("tensor", "sub")),
            P(("tensor", "sub"), "rows"),
            P("groups"),
            P("groups"),
            P(),
            P(("groups", "rows", "tensor", "sub"), None),
        ),
        out_specs=(P(("groups", "tensor", "sub"), "rows"), P(("groups", "rows", "tensor", "sub"))),
        check_vma=False,
    )
```

```python
import functools
import math

import jax
import jax.numpy as jnp
from jax import lax
from jax.experimental import pallas as pl
from jax.experimental.pallas import tpu as pltpu
from jax.sharding import PartitionSpec as P

MESH = pl.DeviceIdType.MESH
F32 = jnp.float32
BF16 = jnp.bfloat16
CHUNKS = 4


def kernel(
    R, T, S,
    counts_in, order_in, gain_in, feat_in, w_in, target_in,
    feat_out, grad_out, loss_out,
    counts_ref, order_ref, gain_ref,
    feat, w, acc, rs, xs, tall, hid, tsel, rowsum, stats, ag, lp, lz, lm,
    w_sem, own_sem, out_sem, f_send, f_recv, rs_send, rs_recv, xs_send, xs_recv,
    tz_send, tz_recv, tm_send, tm_recv, st_send, st_recv,
    ag_send, ag_recv, lz_send, lz_recv, lm_send, lm_recv, tl_sem,
):
    M = T * S
    rows = feat.shape[2]
    part = feat.shape[3]
    cols = w.shape[2]
    pm = rows // S
    mine = R * pm
    share = target_in.shape[0]
    cap = share * M
    total = order_in.shape[1]
    z = lax.axis_index("rows")
    t = lax.axis_index("tensor")
    s_ = lax.axis_index("sub")
    m = t * S + s_

    def member(j):
        q = lax.rem(m + j, M)
        return q, {"tensor": q // S, "sub": lax.rem(q, S)}

    def core(j):
        q = lax.rem(s_ + j, S)
        return q, {"sub": q}

    def across(j):
        q = lax.rem(t + j, T)
        return q, {"tensor": q}

    def zpeer(j):
        q = lax.rem(z + j, R)
        return q, {"rows": q}

    def each_z(body):
        if R <= 4:
            for j in range(1, R):
                body(j)
        else:
            @pl.loop(1, R)
            def _(j):
                body(j)

    def w_copy(q):
        return pltpu.make_async_copy(w_in.at[pl.ds(q * part, part)], w.at[q], w_sem.at[q])

    def own_copy(q):
        return pltpu.make_async_copy(
            feat_in.at[:, pl.ds(q * part, part)], feat.at[z, q], own_sem.at[q])

    for q in range(CHUNKS):
        own_copy(q).start()
    own_cols = pl.ds(pl.multiple_of(z * cols, 128), cols)
    own_t = pltpu.make_async_copy(target_in.at[:, own_cols], tall.at[m, z], tl_sem.at[0])
    own_t.start()
    small = (
        pltpu.make_async_copy(counts_in, counts_ref, tl_sem.at[1]),
        pltpu.make_async_copy(order_in, order_ref, tl_sem.at[2]),
        pltpu.make_async_copy(gain_in.at[:, own_cols], gain_ref, tl_sem.at[3]),
    )
    for c in small:
        c.start()
    for q in range(CHUNKS):
        w_copy(q).start()

    barrier = pltpu.get_barrier_semaphore()

    def hello(j):
        _, dev = zpeer(j)
        pl.semaphore_signal(barrier, inc=1, device_id=dev, device_id_type=MESH)

    each_z(hello)
    for j in range(1, M):
        _, dev = member(j)
        pl.semaphore_signal(barrier, inc=1, device_id=dev, device_id_type=MESH)
    pl.semaphore_wait(barrier, R - 1 + M - 1)

    def f_copy(way, s, q):
        to = jnp.clip(z - 1 if way == 0 else z + 1, 0, R - 1)
        return pltpu.make_async_remote_copy(
            src_ref=feat.at[s, q], dst_ref=feat.at[s, q],
            send_sem=f_send.at[way, s, q], recv_sem=f_recv.at[s, q],
            device_id={"rows": to}, device_id_type=MESH)

    def out_copy(s, q):
        return pltpu.make_async_copy(
            feat.at[s, q],
            feat_out.at[pl.ds(pl.multiple_of(s * rows, rows), rows), pl.ds(q * part, part)],
            out_sem.at[s, q])

    def tz_copy(src, dst, dev):
        columns = pl.ds(pl.multiple_of(dst * cols, 128), cols)
        return pltpu.make_async_remote_copy(
            src_ref=target_in.at[:, columns], dst_ref=tall.at[m, src],
            send_sem=tz_send.at[dst], recv_sem=tz_recv.at[src],
            device_id=dev, device_id_type=MESH)

    def tm_copy(src, dst, dev):
        return pltpu.make_async_remote_copy(
            src_ref=tall.at[src], dst_ref=tall.at[src],
            send_sem=tm_send.at[dst], recv_sem=tm_recv.at[src],
            device_id=dev, device_id_type=MESH)

    def rs_copy(s, src, dst, dev):
        return pltpu.make_async_remote_copy(
            src_ref=acc.at[s, pl.ds(pl.multiple_of(dst * pm, pm), pm)], dst_ref=rs.at[s, src],
            send_sem=rs_send.at[s, dst], recv_sem=rs_recv.at[s, src],
            device_id=dev, device_id_type=MESH)

    def xs_copy(s, src, dst, dev):
        return pltpu.make_async_remote_copy(
            src_ref=xs.at[s, src], dst_ref=xs.at[s, src],
            send_sem=xs_send.at[s, dst], recv_sem=xs_recv.at[s, src],
            device_id=dev, device_id_type=MESH)

    def st_copy(src, dst, dev):
        return pltpu.make_async_remote_copy(
            src_ref=stats.at[src], dst_ref=stats.at[src],
            send_sem=st_send.at[dst], recv_sem=st_recv.at[src],
            device_id=dev, device_id_type=MESH)

    def ag_copy(src, dst, dev):
        return pltpu.make_async_remote_copy(
            src_ref=ag.at[src], dst_ref=ag.at[src],
            send_sem=ag_send.at[dst], recv_sem=ag_recv.at[src],
            device_id=dev, device_id_type=MESH)

    def lz_copy(src, dst, dev):
        return pltpu.make_async_remote_copy(
            src_ref=lp.at[dst], dst_ref=lz.at[src],
            send_sem=lz_send.at[dst], recv_sem=lz_recv.at[src],
            device_id=dev, device_id_type=MESH)

    def lm_copy(src, dst, dev):
        return pltpu.make_async_remote_copy(
            src_ref=lm.at[src], dst_ref=lm.at[src],
            send_sem=lm_send.at[dst], recv_sem=lm_recv.at[src],
            device_id=dev, device_id_type=MESH)

    for q in range(CHUNKS):
        own_copy(q).wait()

        @pl.when(z > 0)
        def _():
            f_copy(0, z, q).start()

        @pl.when(z < R - 1)
        def _():
            f_copy(1, z, q).start()

        out_copy(z, q).start()

    def send_target(j):
        dst, dev = zpeer(j)
        tz_copy(z, dst, dev).start()

    each_z(send_target)

    def multiply(s, q):
        piece = jnp.dot(feat[s, q], w[q], preferred_element_type=F32)
        if q == 0:
            acc[s] = piece
        else:
            acc[s] += piece

    def send_sums(s):
        for j in range(1, S):
            dst, dev = core(j)
            rs_copy(s, s_, dst, dev).start()

    def cross(s):
        h = acc[s, pl.ds(pl.multiple_of(s_ * pm, pm), pm)]
        for j in range(1, S):
            src, dev = core(j)
            rs_copy(s, src, s_, dev).wait_recv()
            h = h + rs[s, src]
        xs[s, t] = h
        for j in range(1, T):
            dst, dev = across(j)
            xs_copy(s, t, dst, dev).start()

    def cross_step(d):
        if isinstance(d, int) and d == 0:
            cross(z)
            return

        @pl.when(z - d >= 0)
        def _():
            cross(z - d)

        @pl.when(z + d < R)
        def _():
            cross(z + d)

    for q in range(CHUNKS):
        w_copy(q).wait()
        multiply(z, q)
    send_sums(z)

    def step(d):
        left, right = z - d, z + d
        for q in range(CHUNKS):
            @pl.when(right < R)
            def _():
                f_copy(0, right, q).wait_recv()

                @pl.when(z > 0)
                def _():
                    f_copy(0, right, q).start()

                out_copy(right, q).start()

            @pl.when(left >= 0)
            def _():
                f_copy(1, left, q).wait_recv()

                @pl.when(z < R - 1)
                def _():
                    f_copy(1, left, q).start()

                out_copy(left, q).start()
                multiply(left, q)

            @pl.when(right < R)
            def _():
                multiply(right, q)

            if q == 0:
                cross_step(d - 1)

        @pl.when(left >= 0)
        def _():
            send_sums(left)

        @pl.when(right < R)
        def _():
            send_sums(right)

    def target_out():
        own_t.wait()

        def arrived(j):
            src, dev = zpeer(j)
            tz_copy(src, z, dev).wait_recv()

        each_z(arrived)
        for j in range(1, M):
            dst, dev = member(j)
            tm_copy(m, dst, dev).start()

    step(1)
    for c in small:
        c.wait()
    target_out()

    row = lax.broadcasted_iota(jnp.int32, (mine, total), 0)
    position = (row // pm) * rows + s_ * pm + lax.rem(row, pm)
    rank = lax.broadcasted_iota(jnp.int32, (1, total), 1)
    trainer = jnp.zeros((1, total), jnp.int32)
    start = jnp.zeros((1, total), jnp.int32)
    end = jnp.int32(0)
    for r in range(R):
        n = counts_ref[r]
        end = end + n
        past = rank >= end
        trainer = trainer + jnp.where(past, 1, 0)
        start = start + jnp.where(past, n, 0)
    natural = trainer * cap + rank - start
    slot = jnp.sum(jnp.where(order_ref[...] == position, natural, 0), axis=1, keepdims=True)

    def step_loop(d, c):
        step(d)
        return c

    if R > 3:
        lax.fori_loop(2, R - 1, step_loop, 0)

    for j in range(1, M):
        src, dev = member(j)
        tm_copy(src, m, dev).wait_recv()
    trn = slot // cap
    inside = slot - trn * cap
    owner = inside // share
    place = owner * (R * share) + trn * share + (inside - owner * share)
    seat = lax.broadcasted_iota(jnp.int32, (mine, M * R * share), 1)
    pick = jnp.where(seat == place, F32(1), F32(0)).astype(BF16)
    tsel[...] = jnp.dot(
        pick, tall[...].reshape(M * R * share, cols), preferred_element_type=F32)

    if R > 2:
        step(R - 1)
    cross_step(R - 1)

    gain = gain_ref[...]
    lane = lax.broadcasted_iota(jnp.int32, (pm, 128), 1)

    def collect(s, c):
        for j in range(1, T):
            src, dev = across(j)
            xs_copy(s, src, t, dev).wait_recv()
        h = xs[s, 0]
        for q in range(1, T):
            h = h + xs[s, q]
        here = pl.ds(pl.multiple_of(s * pm, pm), pm)
        hid[here] = h
        gh = gain * h
        a = jnp.sum(h * h, axis=1, keepdims=True)
        b = jnp.sum(gh * gh, axis=1, keepdims=True)
        e = jnp.sum(gh * tsel[here], axis=1, keepdims=True)
        rowsum[here] = jnp.where(lane == 0, a, jnp.where(lane == 1, b, e))
        return c

    lax.fori_loop(0, R, collect, 0)

    stats[z] = rowsum[...].T[0:8]

    def send_stats(j):
        dst, dev = zpeer(j)
        st_copy(z, dst, dev).start()

    each_z(send_stats)

    def got_stats(j):
        src, dev = zpeer(j)
        st_copy(src, z, dev).wait_recv()

    each_z(got_stats)
    summed = jnp.sum(stats[...], axis=0)
    depth = R * cols
    a, b, e = summed[0:1], summed[1:2], summed[2:3]
    rstat = lax.rsqrt(a / depth + 1e-06)
    scale = 1.0 / math.sqrt(total)
    dotted = (rstat * b - e) * (scale / depth)
    line = lax.broadcasted_iota(jnp.int32, (128, mine), 0)
    factor = jnp.where(line == 0, rstat, rstat * rstat * rstat * dotted).T
    rstat, pull = factor[:, 0:1], factor[:, 1:2]
    h = hid[...]
    err = h * rstat * gain - tsel[...]
    loss = jnp.sum(err * err, axis=1, keepdims=True) / depth
    seat1 = lax.broadcasted_iota(jnp.int32, (mine, cap), 1)

    def scatter(r, c):
        one = jnp.sum(
            jnp.where(slot - r * cap == seat1, loss, F32(0)), axis=0, keepdims=True)
        lp[r] = jnp.broadcast_to(one, (8, cap))
        return c

    lax.fori_loop(0, R, scatter, 0)

    def send_loss(j):
        dst, dev = zpeer(j)
        lz_copy(z, dst, dev).start()

    each_z(send_loss)
    dh = rstat * (gain * (err * scale)) - h * pull
    ag[s_] = dh.astype(BF16)
    for j in range(1, S):
        dst, dev = core(j)
        ag_copy(s_, dst, dev).start()

    lz[z] = lp[z]

    def got_loss(j):
        src, dev = zpeer(j)
        lz_copy(src, z, dev).wait_recv()

    each_z(got_loss)
    lm[s_] = jnp.sum(lz[...], axis=0)
    for j in range(1, S):
        dst, dev = core(j)
        lm_copy(s_, dst, dev).start()

    for j in range(1, S):
        src, dev = core(j)
        ag_copy(src, s_, dev).wait_recv()
    for q in range(S):
        for s in range(R):
            grad_out[s * rows + q * pm:s * rows + (q + 1) * pm] = ag[q, s * pm:(s + 1) * pm]
    for j in range(1, S):
        src, dev = core(j)
        lm_copy(src, s_, dev).wait_recv()
    loss_out[...] = jnp.sum(lm[...], axis=0)

    def sent(s, c):
        for q in range(CHUNKS):
            out_copy(s, q).wait()

            @pl.when(jnp.logical_and(s >= z, z > 0))
            def _():
                f_copy(0, s, q).wait_send()

            @pl.when(jnp.logical_and(s <= z, z < R - 1))
            def _():
                f_copy(1, s, q).wait_send()

        for j in range(1, S):
            dst, dev = core(j)
            rs_copy(s, s_, dst, dev).wait_send()
        for j in range(1, T):
            dst, dev = across(j)
            xs_copy(s, t, dst, dev).wait_send()
        return c

    lax.fori_loop(0, R, sent, 0)
    for j in range(1, M):
        dst, dev = member(j)
        tm_copy(m, dst, dev).wait_send()
    for j in range(1, S):
        dst, dev = core(j)
        ag_copy(s_, dst, dev).wait_send()
        lm_copy(s_, dst, dev).wait_send()

    def sent_z(j):
        dst, dev = zpeer(j)
        tz_copy(z, dst, dev).wait_send()
        st_copy(z, dst, dev).wait_send()
        lz_copy(z, dst, dev).wait_send()

    each_z(sent_z)


def outer(f_ref, g_ref, out_ref):
    out_ref[...] = lax.dot_general(
        f_ref[...], g_ref[...], (((0,), (0,)), ((), ())), preferred_element_type=F32)


def on_device(features, fc_weight, counts, order, norm_gain, target):
    R = lax.axis_size("rows")
    T = lax.axis_size("tensor")
    S = lax.axis_size("sub")
    M = T * S
    rows, depth = features.shape
    cols = fc_weight.shape[1]
    total = order.shape[0]
    share = target.shape[0]
    cap = share * M
    part = depth // CHUNKS
    pm = rows // S
    mine = R * pm
    any_ = pl.BlockSpec(memory_space=pl.ANY)
    hbm = pl.BlockSpec(memory_space=pltpu.HBM)
    vmem = pl.BlockSpec(memory_space=pltpu.VMEM)
    dma = pltpu.SemaphoreType.DMA
    all_features, grad, loss = pl.pallas_call(
        functools.partial(kernel, R, T, S),
        out_shape=(
            jax.ShapeDtypeStruct((total, depth), BF16),
            jax.ShapeDtypeStruct((total, cols), BF16),
            jax.ShapeDtypeStruct((8, cap), F32),
        ),
        in_specs=[hbm] * 6,
        out_specs=(any_, vmem, vmem),
        scratch_shapes=[
            pltpu.SMEM((R,), jnp.int32),
            pltpu.VMEM((1, total), jnp.int32),
            pltpu.VMEM((1, cols), F32),
            pltpu.VMEM((R, CHUNKS, rows, part), BF16),
            pltpu.VMEM((CHUNKS, part, cols), BF16),
            pltpu.VMEM((R, rows, cols), F32),
            pltpu.VMEM((R, S, pm, cols), F32),
            pltpu.VMEM((R, T, pm, cols), F32),
            pltpu.VMEM((M, R, share, cols), BF16),
            pltpu.VMEM((mine, cols), F32),
            pltpu.VMEM((mine, cols), F32),
            pltpu.VMEM((mine, 128), F32),
            pltpu.VMEM((R, 8, mine), F32),
            pltpu.VMEM((S, mine, cols), BF16),
            pltpu.VMEM((R, 8, cap), F32),
            pltpu.VMEM((R, 8, cap), F32),
            pltpu.VMEM((S, 8, cap), F32),
            dma((CHUNKS,)), dma((CHUNKS,)), dma((R, CHUNKS)),
            dma((2, R, CHUNKS)), dma((R, CHUNKS)),
            dma((R, S)), dma((R, S)), dma((R, T)), dma((R, T)),
            dma((R,)), dma((R,)), dma((M,)), dma((M,)),
            dma((R,)), dma((R,)), dma((S,)), dma((S,)),
            dma((R,)), dma((R,)), dma((S,)), dma((S,)), dma((4,)),
        ],
        compiler_params=pltpu.CompilerParams(
            collective_id=0, has_side_effects=True, vmem_limit_bytes=60 * 1024 * 1024),
        name="gather_join_norm",
    )(counts, order[None, :], norm_gain[None, :], features, fc_weight, target)
    member = lax.axis_index("tensor") * S + lax.axis_index("sub")
    loss_slots = lax.dynamic_slice_in_dim(loss[0], member * share, share, 0)
    tile = depth // 4
    fc_grad = pl.pallas_call(
        outer,
        grid=(depth // tile,),
        out_shape=jax.ShapeDtypeStruct((depth, cols), F32),
        in_specs=[
            pl.BlockSpec((total, tile), lambda i: (0, i)),
            pl.BlockSpec((total, cols), lambda i: (0, 0)),
        ],
        out_specs=pl.BlockSpec((tile, cols), lambda i: (i, 0)),
        compiler_params=pltpu.CompilerParams(vmem_limit_bytes=32 * 1024 * 1024),
        name="weight_gradient",
    )(all_features, grad)
    return (fc_grad, loss_slots)


def solution(mesh):
    return jax.shard_map(
        on_device,
        mesh=mesh,
        in_specs=(
            P(("groups", "rows"), ("tensor", "sub")),
            P(("tensor", "sub"), "rows"),
            P("groups"),
            P("groups"),
            P(),
            P(("groups", "rows", "tensor", "sub"), None),
        ),
        out_specs=(P(("groups", "tensor", "sub"), "rows"), P(("groups", "rows", "tensor", "sub"))),
        check_vma=False,
    )
```
